1024 devices in a mesh: domain: 128 (over z, y_lo, core), band: 8 (over x, y_hi).
Axes of the slice: x: 4, y: 8 (y_hi: 2, y_lo: 4; y = y_hi * 4 + y_lo), z: 16, core: 2. Of those that a mesh axis runs over, the one named last changes fastest.
Arguments:
- orbitals: bfloat16 [256, 256, 8, 128], P('band', 'domain'), may hold values from -6 to 6
- potential: float32 [256, 8, 128], P('domain'), may hold values from -1 to 1.5
Outputs:
- filtered: bfloat16 [256, 256, 8, 128], P('band', 'domain')
- margin_rows: float32 [256, 256], P('band')
- projected_rows: float32 [256, 256], P('band')
The draws below stay inside these ranges and needn't reach their ends.
All inputs are finite; a program needn't handle non-finite values.
Results may differ from the reference program's by a relative error of at most 0.003.
Values may be sent and summed in bfloat16 or wider, within the bound.
A program may use at most 32 MiB of HBM per device.

```python
import jax
import jax.numpy as jnp
from jax import lax

NB = 32
NY = 8
NZ = 128
NX = 256
ORBITALS = 256
N_BAND = 8


def levels(rng, shape, cuts, smallest, largest):
    loudness, own = 1.0, jax.random.fold_in(rng, 6)
    for axis_at, blocks in cuts:
        steps = jnp.exp(jax.random.uniform(jax.random.fold_in(own, axis_at), (blocks,), jnp.float32, smallest / len(cuts), largest / len(cuts)))
        loudness = loudness * jnp.repeat(steps, shape[axis_at] // blocks).reshape([-1 if axis == axis_at else 1 for axis in range(len(shape))])
    return loudness


def scatter_about(key, shape, width, most, split=(), dtype=jnp.bfloat16):
    level = levels(key, shape, split, -0.22, 0.18) if split else 1.0
    entries = jax.random.normal(key, shape, jnp.float32) * width * level
    return jnp.minimum(jnp.maximum(entries, -most), most).astype(dtype)


def setup_inputs(seed: int = 0) -> dict:
    seeds = jax.random.split(jax.random.key(seed), 3)
    return {
        "orbitals": scatter_about(seeds[0], (ORBITALS, NX, NY, NZ), 1.0, 6.0, ((0, 8), (1, 128))),
        "potential": jnp.clip(-1.0 + 2.5 * jax.random.uniform(seeds[1], (NX, NY, NZ), jnp.float32) ** levels(seeds[1], (NX, NY, NZ), ((0, 128),), -0.2, 0.2), -1.0, 1.5),
    }


LOWER = -1.0
CUTOFF = 1.0
UPPER = 7.5


def filter_terms():
    half_width = (UPPER - CUTOFF) / 2.0
    center = (UPPER + CUTOFF) / 2.0
    sigma = half_width / (LOWER - center)
    gamma = 2.0 / sigma
    terms = [(sigma / half_width, 0.0)]
    for step in range(3):
        sigma_next = 1.0 / (gamma - sigma)
        terms.append((2.0 * sigma_next / half_width, sigma * sigma_next))
        sigma = sigma_next
    return center, terms


def hamil(field, potential):
    near = jnp.roll(field, -1, 1) + jnp.roll(field, 1, 1)
    near = near + jnp.roll(field, 1, 2) + jnp.roll(field, -1, 2)
    near = near + jnp.roll(field, 1, 3) + jnp.roll(field, -1, 3)
    return -0.5 * (near - 6.0 * field) + potential[None] * field


def reference(orbitals, potential):
    center, terms = filter_terms()
    blocks = orbitals.reshape(N_BAND, NB, NX, NY, NZ)

    def filter_block(block):
        prior = block.astype(jnp.float32)
        current = terms[0][0] * (hamil(prior, potential) - center * prior)
        for alpha, beta in terms[1:]:
            update = alpha * (hamil(current, potential) - center * current) - beta * prior
            prior, current = current, update
        return current.astype(jnp.bfloat16)

    filtered = lax.map(filter_block, blocks)

    def apply_block(block):
        return hamil(block.astype(jnp.float32), potential).astype(jnp.bfloat16)

    applied = lax.map(apply_block, filtered)
    flat_y = filtered.reshape(NB * N_BAND, NX * NY * NZ).astype(jnp.float32)
    flat_h = applied.reshape(NB * N_BAND, NX * NY * NZ).astype(jnp.float32)
    scale = 1.0 / (NX * NY * NZ)
    dims = (((1,), (1,)), ((), ()))
    margin_rows = lax.dot_general(flat_y, flat_y, dims, precision=lax.Precision.HIGHEST, preferred_element_type=jnp.float32) * scale
    projected_rows = lax.dot_general(flat_h, flat_y, dims, precision=lax.Precision.HIGHEST, preferred_element_type=jnp.float32) * scale
    return filtered.reshape(NB * N_BAND, NX, NY, NZ), margin_rows, projected_rows
```

```python
import functools

import jax
import jax.numpy as jnp
from jax import lax
from jax.experimental import pallas as pl
from jax.experimental.pallas import tpu as pltpu
from jax.sharding import PartitionSpec as P

MESH = pl.DeviceIdType.MESH
LOWER = -1.0
CUTOFF = 1.0
UPPER = 7.5
F32 = jnp.float32
BF16 = jnp.bfloat16
GROUP = 8
NB = 32
NY = 8
NZ = 128
CHUNKS = 4
HALVES = 2


def filter_terms():
    half_width = (UPPER - CUTOFF) / 2.0
    center = (UPPER + CUTOFF) / 2.0
    sigma = half_width / (LOWER - center)
    gamma = 2.0 / sigma
    terms = [(sigma / half_width, 0.0)]
    for step in range(3):
        sigma_next = 1.0 / (gamma - sigma)
        terms.append((2.0 * sigma_next / half_width, sigma * sigma_next))
        sigma = sigma_next
    return center, terms


def side_sum(plane):
    return (
        (pltpu.roll(plane, 1, 0) + pltpu.roll(plane, NY - 1, 0))
        + (pltpu.roll(plane, 1, 1) + pltpu.roll(plane, NZ - 1, 1))
    )


def kernel(
    n_domain, scale,
    x_hbm, v_ref,
    y_ref, g_ref,
    xs, vs, ws, zst, hst, halo_out, halo_in, zall, lhs, gsum, rsb, zb, fin,
    lsem, xss, xrs, vss, vrs, hss, hrs, bss, brs, fss, frs, rss, rrs, zss, zrs, ass, ars,
):
    n_z = n_domain // GROUP
    d = lax.axis_index("domain")
    b = lax.axis_index("band")
    z, j = d // GROUP, d % GROUP
    x, h = b // 2, b % 2

    def at_d(step):
        return (lax.rem(d + step + n_domain, n_domain), b)

    def at_g(step):
        return (z * GROUP + lax.rem(j + step + GROUP, GROUP), b)

    def at_z(step):
        return (lax.rem(z + step + n_z, n_z) * GROUP + j, b)

    def at_b(dx, dh):
        return (d, lax.rem(x + dx + 4, 4) * 2 + lax.rem(h + dh, 2))

    def remote(src, dst, send, recv, to):
        return pltpu.make_async_remote_copy(
            src_ref=src, dst_ref=dst, send_sem=send, recv_sem=recv, device_id=to, device_id_type=MESH
        )

    own = pltpu.make_async_copy(x_hbm, xs.at[2], lsem)
    own.start()
    barrier = pltpu.get_barrier_semaphore()
    partners = [at_d(s) for s in (-2, -1, 1, 2)] + [at_g(s) for s in range(1, GROUP)] + [at_z(-1), at_z(1)]
    partners += [at_b(0, 1), at_b(1, 0), at_b(-1, 0), at_b(2, 0)]
    for to in partners:
        pl.semaphore_signal(barrier, inc=1, device_id=to, device_id_type=MESH)
    vs[2] = v_ref[...]
    own.wait()
    pl.semaphore_wait(barrier, len(partners))

    pending = []
    shifts = (-1, 1, -2, 2)
    v_in = []
    for n, s in enumerate(shifts):
        cp = remote(vs.at[2], vs.at[2 - s], vss.at[n], vrs.at[n], at_d(s))
        cp.start()
        v_in.append(cp)
    pending += v_in
    size = NB // CHUNKS
    x_in = []
    for c in range(CHUNKS):
        part = pl.ds(c * size, size)
        x_in.append([])
        for n, s in enumerate(shifts):
            cp = remote(xs.at[2, part], xs.at[2 - s, part], xss.at[n, c], xrs.at[n, c], at_d(s))
            cp.start()
            x_in[c].append(cp)
        pending += x_in[c]

    center, terms = filter_terms()
    for cp in v_in:
        cp.wait_recv()
    for k, (alpha, _) in enumerate(terms):
        for p in range(k + 1, 9 - k):
            ws[k, p] = alpha * (vs[p // 2, (p % 2) * NY:(p % 2) * NY + NY, :] + (3.0 - center))

    def filter_one(o):
        prior = {}
        for s in range(5):
            block = xs[s, o].astype(F32)
            prior[2 * s], prior[2 * s + 1] = block[:NY], block[NY:]
        current = None
        for k, (alpha, beta) in enumerate(terms):
            base = prior if k == 0 else current
            update = {}
            for p in range(k + 1, 9 - k):
                near = side_sum(base[p]) + (base[p - 1] + base[p + 1])
                value = ws[k, p] * base[p] - (0.5 * alpha) * near
                if k:
                    value = value - beta * prior[p]
                update[p] = value
            if k:
                prior = current
            current = update
        zst[0, pl.ds(o, NY, stride=NB), :] = current[4]
        zst[1, pl.ds(o, NY, stride=NB), :] = current[5]
        y_ref[o] = jnp.concatenate([current[4], current[5]], axis=0).astype(BF16)
        return current[4], current[5]

    def filter_pair(i, _):
        low0, high0 = filter_one(2 * i)
        low1, high1 = filter_one(2 * i + 1)
        halo_out[0, i] = jnp.concatenate([low0, low1], axis=0).astype(BF16)
        halo_out[1, i] = jnp.concatenate([high0, high1], axis=0).astype(BF16)
        return 0

    me = 32 * b
    mate = 32 * (x * 2 + (1 - h))
    x_steps = (1, -1, 2)
    half = NB // HALVES
    band_in, fwd_in, mate_in = [], [], []
    for t in range(HALVES):
        for c in range(t * CHUNKS // HALVES, (t + 1) * CHUNKS // HALVES):
            for cp in x_in[c]:
                cp.wait_recv()
            lax.fori_loop(c * size // 2, (c + 1) * size // 2, filter_pair, 0)
        rows = pl.ds(pl.multiple_of(me + t * half, 16), half)
        for y in range(NY):
            for p in range(2):
                piece = zst[p, y * NB + t * half:y * NB + (t + 1) * half, :].astype(BF16)
                zall[y, rows, p * NZ:(p + 1) * NZ] = piece
                lhs[y, t * half:(t + 1) * half, p * NZ:(p + 1) * NZ] = piece
        piece = zall.at[:, rows, :]
        cp = remote(piece, piece, bss.at[0, t], brs.at[0, t], at_b(0, 1))
        cp.start()
        mate_in.append(cp)
        for n, s in enumerate(x_steps):
            cp = remote(piece, piece, bss.at[n + 1, t], brs.at[n + 1, t], at_b(s, 0))
            cp.start()
            band_in.append(cp)
    pending += mate_in + band_in

    h_in = []
    for n, s in enumerate((-1, 1)):
        cp = remote(halo_out.at[n], halo_in.at[1 - n], hss.at[n], hrs.at[n], at_d(s))
        cp.start()
        h_in.append(cp)
    pending += h_in

    for t in range(HALVES):
        mate_in[t].wait_recv()
        piece = zall.at[:, pl.ds(pl.multiple_of(mate + t * half, 16), half), :]
        for n, s in enumerate(x_steps):
            cp = remote(piece, piece, fss.at[n, t], frs.at[n, t], at_b(s, 0))
            cp.start()
            fwd_in.append(cp)
    pending += fwd_in

    for cp in h_in:
        cp.wait_recv()

    def apply_pair(i, _):
        left, right = halo_in[0, i].astype(F32), halo_in[1, i].astype(F32)
        for q in range(2):
            o = 2 * i + q
            block = y_ref[o].astype(F32)
            planes = (left[q * NY:(q + 1) * NY], block[:NY], block[NY:], right[q * NY:(q + 1) * NY])
            for p in (1, 2):
                near = (planes[p - 1] + planes[p + 1]) + side_sum(planes[p])
                value = -0.5 * (near - 6.0 * planes[p]) + v_ref[(p - 1) * NY:p * NY, :] * planes[p]
                hst[p - 1, pl.ds(o, NY, stride=NB), :] = value
        return 0

    lax.fori_loop(0, NB // 2, apply_pair, 0)
    for y in range(NY):
        for p in range(2):
            lhs[y, NB:2 * NB, p * NZ:(p + 1) * NZ] = hst[p, y * NB:(y + 1) * NB, :].astype(BF16)

    for cp in band_in + fwd_in:
        cp.wait_recv()
    total = None
    for y in range(NY):
        term = lax.dot_general(lhs[y], zall[y], (((1,), (1,)), ((), ())), preferred_element_type=F32)
        total = term if total is None else total + term
    gsum[...] = total

    r_in = []
    for s in range(1, GROUP):
        there = lax.rem(j + s, GROUP)
        cp = remote(gsum.at[pl.ds(pl.multiple_of(there * 8, 8), 8)], rsb.at[s], rss.at[s], rrs.at[s], at_g(s))
        cp.start()
        r_in.append(cp)
    pending += r_in
    mine = pl.ds(pl.multiple_of(j * 8, 8), 8)
    shard = gsum[mine, :]
    for s in range(1, GROUP):
        r_in[s - 1].wait_recv()
        shard = shard + rsb[s]
    zb[z] = shard

    up, down = n_z // 2, (n_z - 1) // 2

    def hop(way, k):
        origin = lax.rem(z - way * k + n_z, n_z)
        n = (way + 1) // 2
        cp = remote(zb.at[origin], zb.at[origin], zss.at[n, k], zrs.at[n, k], at_z(way))
        cp.start()
        return cp

    ups, downs = [hop(1, 0)], [hop(-1, 0)]
    for k in range(1, up):
        ups[-1].wait_recv()
        ups.append(hop(1, k))
    for k in range(1, down):
        downs[-1].wait_recv()
        downs.append(hop(-1, k))
    ups[-1].wait_recv()
    downs[-1].wait_recv()
    pending += ups + downs
    values = [zb[k] for k in range(n_z)]
    while len(values) > 1:
        values = [values[k] + values[k + 1] for k in range(0, len(values), 2)]
    fin[mine, :] = values[0] * scale

    a_in = []
    for s in range(1, GROUP):
        cp = remote(fin.at[mine], fin.at[mine], ass.at[s], ars.at[s], at_g(s))
        cp.start()
        a_in.append(cp)
    for cp in a_in:
        cp.wait_recv()
    pending += a_in
    g_ref[...] = fin[...]
    for cp in pending:
        cp.wait_send()


def shards(orbitals, potential, n_domain, n_band):
    n_z = n_domain // GROUP
    half_z = n_z // 2
    block = orbitals.reshape(NB, 2 * NY, NZ)
    scale = 1.0 / (n_domain * 2 * NY * NZ)
    dma = pltpu.SemaphoreType.DMA
    vmem = pl.BlockSpec(memory_space=pltpu.VMEM)
    filtered, rows = pl.pallas_call(
        functools.partial(kernel, n_domain, scale),
        out_shape=(
            jax.ShapeDtypeStruct((NB, 2 * NY, NZ), BF16),
            jax.ShapeDtypeStruct((2 * NB, n_band * NB), F32),
        ),
        in_specs=[pl.BlockSpec(memory_space=pl.ANY), vmem],
        out_specs=(vmem, vmem),
        scratch_shapes=[
            pltpu.VMEM((5, NB, 2 * NY, NZ), BF16),
            pltpu.VMEM((5, 2 * NY, NZ), F32),
            pltpu.VMEM((4, 10, NY, NZ), F32),
            pltpu.VMEM((2, NY * NB, NZ), F32),
            pltpu.VMEM((2, NY * NB, NZ), F32),
            pltpu.VMEM((2, NB // 2, 2 * NY, NZ), BF16),
            pltpu.VMEM((2, NB // 2, 2 * NY, NZ), BF16),
            pltpu.VMEM((NY, n_band * NB, 2 * NZ), BF16),
            pltpu.VMEM((NY, 2 * NB, 2 * NZ), BF16),
            pltpu.VMEM((2 * NB, n_band * NB), F32),
            pltpu.VMEM((GROUP, 8, n_band * NB), F32),
            pltpu.VMEM((n_z, 8, n_band * NB), F32),
            pltpu.VMEM((2 * NB, n_band * NB), F32),
            dma,
            dma((4, CHUNKS)), dma((4, CHUNKS)),
            dma((4,)), dma((4,)),
            dma((2,)), dma((2,)),
            dma((4, HALVES)), dma((4, HALVES)),
            dma((3, HALVES)), dma((3, HALVES)),
            dma((GROUP,)), dma((GROUP,)),
            dma((2, half_z)), dma((2, half_z)),
            dma((GROUP,)), dma((GROUP,)),
        ],
        compiler_params=pltpu.CompilerParams(
            collective_id=1, has_side_effects=True, vmem_limit_bytes=24 * 1024 * 1024
        ),
    )(block, potential.reshape(2 * NY, NZ))
    return filtered.reshape(orbitals.shape), rows[:NB], rows[NB:]


def solution(mesh):
    body = functools.partial(shards, n_domain=mesh.shape["domain"], n_band=mesh.shape["band"])
    in_specs = (P("band", "domain", None, None), P("domain", None, None))
    out_specs = (P("band", "domain", None, None), P("band", None), P("band", None))
    return jax.shard_map(body, mesh=mesh, in_specs=in_specs, out_specs=out_specs, check_vma=False)
```

```python
import functools

import jax
import jax.numpy as jnp
from jax import lax
from jax.experimental import pallas as pl
from jax.experimental.pallas import tpu as pltpu
from jax.sharding import PartitionSpec as P

MESH = pl.DeviceIdType.MESH
LOWER = -1.0
CUTOFF = 1.0
UPPER = 7.5
F32 = jnp.float32
BF16 = jnp.bfloat16
GROUP = 8
NB = 32
NY = 8
NZ = 128
CHUNKS = 4
HALVES = 2
BATCH = 4


def filter_terms():
    half_width = (UPPER - CUTOFF) / 2.0
    center = (UPPER + CUTOFF) / 2.0
    sigma = half_width / (LOWER - center)
    gamma = 2.0 / sigma
    terms = [(sigma / half_width, 0.0)]
    for step in range(3):
        sigma_next = 1.0 / (gamma - sigma)
        terms.append((2.0 * sigma_next / half_width, sigma * sigma_next))
        sigma = sigma_next
    return center, terms


def side_sum(plane):
    return (
        (pltpu.roll(plane, 1, 0) + pltpu.roll(plane, NY - 1, 0))
        + (pltpu.roll(plane, 1, 1) + pltpu.roll(plane, NZ - 1, 1))
    )


def kernel(
    n_domain, scale,
    x_hbm, v_hbm,
    y_ref, g_ref,
    xs, vs, ws, zst, hst, halo_out, halo_in, zall, lhs, gsum, rsb, zb, fin,
    lsem, xss, xrs, vss, vrs, hss, hrs, bss, brs, fss, frs, rss, rrs, zss, zrs, ass, ars, tokens,
):
    n_z = n_domain // GROUP
    d = lax.axis_index("domain")
    b = lax.axis_index("band")
    z, j = d // GROUP, d % GROUP
    x, h = b // 2, b % 2

    def at_d(step):
        return (lax.rem(d + step + n_domain, n_domain), b)

    def at_g(step):
        return (z * GROUP + lax.rem(j + step + GROUP, GROUP), b)

    def at_z(step):
        return (lax.rem(z + step + n_z, n_z) * GROUP + j, b)

    def at_b(dx, dh):
        return (d, lax.rem(x + dx + 4, 4) * 2 + lax.rem(h + dh, 2))

    def remote(src, dst, send, recv, to):
        return pltpu.make_async_remote_copy(
            src_ref=src, dst_ref=dst, send_sem=send, recv_sem=recv, device_id=to, device_id_type=MESH
        )

    own = pltpu.make_async_copy(x_hbm, xs.at[2], lsem.at[0])
    own_v = pltpu.make_async_copy(v_hbm, vs.at[2], lsem.at[1])
    own.start()
    own_v.start()
    barrier = pltpu.get_barrier_semaphore()
    partners = [at_d(s) for s in (-2, -1, 1, 2)] + [at_g(s) for s in range(1, GROUP)] + [at_z(-1), at_z(1)]
    partners += [at_b(0, 1), at_b(1, 0), at_b(-1, 0), at_b(2, 0)]
    for to in partners:
        pl.semaphore_signal(barrier, inc=1, device_id=to, device_id_type=MESH)
    own.wait()
    own_v.wait()
    pl.semaphore_wait(barrier, len(partners))

    def greet(n):
        for to in (at_z(-(1 << n)), at_z(1 << n)):
            pl.semaphore_signal(tokens.at[n], inc=1, device_id=to, device_id_type=MESH)

    def greeted(n):
        pl.semaphore_wait(tokens.at[n], 2)

    greet(0)

    pending = []
    shifts = (-1, 1, -2, 2)
    v_in = []
    for n, s in enumerate(shifts):
        cp = remote(vs.at[2], vs.at[2 - s], vss.at[n], vrs.at[n], at_d(s))
        cp.start()
        v_in.append(cp)
    pending += v_in
    size = NB // CHUNKS
    x_in = []
    for c in range(CHUNKS):
        part = pl.ds(c * size, size)
        x_in.append([])
        for n, s in enumerate(shifts):
            cp = remote(xs.at[2, part], xs.at[2 - s, part], xss.at[n, c], xrs.at[n, c], at_d(s))
            cp.start()
            x_in[c].append(cp)
        pending += x_in[c]

    center, terms = filter_terms()
    for cp in v_in:
        cp.wait_recv()
    for k, (alpha, _) in enumerate(terms):
        for p in range(k + 1, 9 - k):
            ws[k, p] = alpha * (vs[p // 2, (p % 2) * NY:(p % 2) * NY + NY, :] + (3.0 - center))

    def filter_some(i, _):
        orbitals = [i * BATCH + q for q in range(BATCH)]
        priors, currents = [], [None] * BATCH
        for o in orbitals:
            planes = {}
            for s in range(5):
                block = xs[s, o].astype(F32)
                planes[2 * s], planes[2 * s + 1] = block[:NY], block[NY:]
            priors.append(planes)
        for k, (alpha, beta) in enumerate(terms):
            for q in range(BATCH):
                base = currents[q] if k else priors[q]
                update = {}
                for p in range(k + 1, 9 - k):
                    near = side_sum(base[p]) + (base[p - 1] + base[p + 1])
                    value = ws[k, p] * base[p] - (0.5 * alpha) * near
                    if k:
                        value = value - beta * priors[q][p]
                    update[p] = value
                if k:
                    priors[q] = currents[q]
                currents[q] = update
        for q, o in enumerate(orbitals):
            low, high = currents[q][4], currents[q][5]
            zst[0, pl.ds(o, NY, stride=NB), :] = low
            zst[1, pl.ds(o, NY, stride=NB), :] = high
            y_ref[o] = jnp.concatenate([low, high], axis=0).astype(BF16)
        for q in range(0, BATCH, 2):
            for side in range(2):
                pair = [currents[q + r][4 + side] for r in range(2)]
                halo_out[side, i * (BATCH // 2) + q // 2] = jnp.concatenate(pair, axis=0).astype(BF16)
        return 0

    me = 32 * b
    mate = 32 * (x * 2 + (1 - h))
    x_steps = (1, -1, 2)
    half = NB // HALVES
    band_in, fwd_in, mate_in = [], [], []
    for t in range(HALVES):
        for c in range(t * CHUNKS // HALVES, (t + 1) * CHUNKS // HALVES):
            for cp in x_in[c]:
                cp.wait_recv()
            lax.fori_loop(c * size // BATCH, (c + 1) * size // BATCH, filter_some, 0)
        rows = pl.ds(pl.multiple_of(me + t * half, 16), half)
        for y in range(NY):
            for p in range(2):
                piece = zst[p, y * NB + t * half:y * NB + (t + 1) * half, :].astype(BF16)
                zall[y, rows, p * NZ:(p + 1) * NZ] = piece
                lhs[y, t * half:(t + 1) * half, p * NZ:(p + 1) * NZ] = piece
        piece = zall.at[:, rows, :]
        cp = remote(piece, piece, bss.at[0, t], brs.at[0, t], at_b(0, 1))
        cp.start()
        mate_in.append(cp)
        for n, s in enumerate(x_steps):
            cp = remote(piece, piece, bss.at[n + 1, t], brs.at[n + 1, t], at_b(s, 0))
            cp.start()
            band_in.append(cp)
    pending += mate_in + band_in

    h_in = []
    for n, s in enumerate((-1, 1)):
        cp = remote(halo_out.at[n], halo_in.at[1 - n], hss.at[n], hrs.at[n], at_d(s))
        cp.start()
        h_in.append(cp)
    pending += h_in

    greeted(0)
    greet(1)
    for t in range(HALVES):
        mate_in[t].wait_recv()
        piece = zall.at[:, pl.ds(pl.multiple_of(mate + t * half, 16), half), :]
        for n, s in enumerate(x_steps):
            cp = remote(piece, piece, fss.at[n, t], frs.at[n, t], at_b(s, 0))
            cp.start()
            fwd_in.append(cp)
    pending += fwd_in

    for cp in h_in:
        cp.wait_recv()

    def apply_pair(i, _):
        left, right = halo_in[0, i].astype(F32), halo_in[1, i].astype(F32)
        for q in range(2):
            o = 2 * i + q
            block = y_ref[o].astype(F32)
            planes = (left[q * NY:(q + 1) * NY], block[:NY], block[NY:], right[q * NY:(q + 1) * NY])
            for p in (1, 2):
                near = (planes[p - 1] + planes[p + 1]) + side_sum(planes[p])
                value = -0.5 * (near - 6.0 * planes[p]) + vs[2, (p - 1) * NY:p * NY, :] * planes[p]
                hst[p - 1, pl.ds(o, NY, stride=NB), :] = value
        return 0

    lax.fori_loop(0, NB // 2, apply_pair, 0)
    for y in range(NY):
        for p in range(2):
            lhs[y, NB:2 * NB, p * NZ:(p + 1) * NZ] = hst[p, y * NB:(y + 1) * NB, :].astype(BF16)

    greeted(1)
    greet(2)
    for cp in band_in + fwd_in:
        cp.wait_recv()
    total = None
    for y in range(NY):
        term = lax.dot_general(lhs[y], zall[y], (((1,), (1,)), ((), ())), preferred_element_type=F32)
        total = term if total is None else total + term
    gsum[...] = total

    r_in = []
    for s in range(1, GROUP):
        there = lax.rem(j + s, GROUP)
        cp = remote(gsum.at[pl.ds(pl.multiple_of(there * 8, 8), 8)], rsb.at[s], rss.at[s], rrs.at[s], at_g(s))
        cp.start()
        r_in.append(cp)
    pending += r_in
    mine = pl.ds(pl.multiple_of(j * 8, 8), 8)
    shard = gsum[mine, :]
    for s in range(1, GROUP):
        r_in[s - 1].wait_recv()
        shard = shard + rsb[s]
    zb[z] = shard

    greeted(2)
    z_in = []
    for s in sorted(range(1, n_z), key=lambda s: -min(s, n_z - s)):
        cp = remote(zb.at[z], zb.at[z], zss.at[s], zrs.at[s], at_z(s))
        cp.start()
        z_in.append(cp)
    for cp in z_in:
        cp.wait_recv()
    pending += z_in
    values = [zb[k] for k in range(n_z)]
    while len(values) > 1:
        values = [values[k] + values[k + 1] for k in range(0, len(values), 2)]
    fin[mine, :] = values[0] * scale

    a_in = []
    for s in range(1, GROUP):
        cp = remote(fin.at[mine], fin.at[mine], ass.at[s], ars.at[s], at_g(s))
        cp.start()
        a_in.append(cp)
    for cp in a_in:
        cp.wait_recv()
    pending += a_in
    g_ref[...] = fin[...]
    for cp in pending:
        cp.wait_send()


def shards(orbitals, potential, n_domain, n_band):
    n_z = n_domain // GROUP
    block = orbitals.reshape(NB, 2 * NY, NZ)
    scale = 1.0 / (n_domain * 2 * NY * NZ)
    dma = pltpu.SemaphoreType.DMA
    vmem = pl.BlockSpec(memory_space=pltpu.VMEM)
    filtered, rows = pl.pallas_call(
        functools.partial(kernel, n_domain, scale),
        out_shape=(
            jax.ShapeDtypeStruct((NB, 2 * NY, NZ), BF16),
            jax.ShapeDtypeStruct((2 * NB, n_band * NB), F32),
        ),
        in_specs=[pl.BlockSpec(memory_space=pltpu.HBM)] * 2,
        out_specs=(vmem, vmem),
        scratch_shapes=[
            pltpu.VMEM((5, NB, 2 * NY, NZ), BF16),
            pltpu.VMEM((5, 2 * NY, NZ), F32),
            pltpu.VMEM((4, 10, NY, NZ), F32),
            pltpu.VMEM((2, NY * NB, NZ), F32),
            pltpu.VMEM((2, NY * NB, NZ), F32),
            pltpu.VMEM((2, NB // 2, 2 * NY, NZ), BF16),
            pltpu.VMEM((2, NB // 2, 2 * NY, NZ), BF16),
            pltpu.VMEM((NY, n_band * NB, 2 * NZ), BF16),
            pltpu.VMEM((NY, 2 * NB, 2 * NZ), BF16),
            pltpu.VMEM((2 * NB, n_band * NB), F32),
            pltpu.VMEM((GROUP, 8, n_band * NB), F32),
            pltpu.VMEM((n_z, 8, n_band * NB), F32),
            pltpu.VMEM((2 * NB, n_band * NB), F32),
            dma((2,)),
            dma((4, CHUNKS)), dma((4, CHUNKS)),
            dma((4,)), dma((4,)),
            dma((2,)), dma((2,)),
            dma((4, HALVES)), dma((4, HALVES)),
            dma((3, HALVES)), dma((3, HALVES)),
            dma((GROUP,)), dma((GROUP,)),
            dma((n_z,)), dma((n_z,)),
            dma((GROUP,)), dma((GROUP,)),
            pltpu.SemaphoreType.REGULAR((3,)),
        ],
        compiler_params=pltpu.CompilerParams(
            collective_id=1, has_side_effects=True, vmem_limit_bytes=24 * 1024 * 1024
        ),
    )(block, potential.reshape(2 * NY, NZ))
    return filtered.reshape(orbitals.shape), rows[:NB], rows[NB:]


def solution(mesh):
    body = functools.partial(shards, n_domain=mesh.shape["domain"], n_band=mesh.shape["band"])
    in_specs = (P("band", "domain", None, None), P("domain", None, None))
    out_specs = (P("band", "domain", None, None), P("band", None), P("band", None))
    return jax.shard_map(body, mesh=mesh, in_specs=in_specs, out_specs=out_specs, check_vma=False)
```

```python
import functools

import jax
import jax.numpy as jnp
from jax import lax
from jax.experimental import pallas as pl
from jax.experimental.pallas import tpu as pltpu
from jax.sharding import PartitionSpec as P

MESH = pl.DeviceIdType.MESH
LOWER = -1.0
CUTOFF = 1.0
UPPER = 7.5
F32 = jnp.float32
BF16 = jnp.bfloat16
GROUP = 8
NB = 32
NY = 8
NZ = 128
CHUNKS = 4
HALVES = 2
SPLIT = 2
MATE_FIRST = False
BATCH = 4


def filter_terms():
    half_width = (UPPER - CUTOFF) / 2.0
    center = (UPPER + CUTOFF) / 2.0
    sigma = half_width / (LOWER - center)
    gamma = 2.0 / sigma
    terms = [(sigma / half_width, 0.0)]
    for step in range(3):
        sigma_next = 1.0 / (gamma - sigma)
        terms.append((2.0 * sigma_next / half_width, sigma * sigma_next))
        sigma = sigma_next
    return center, terms


def side_sum(plane):
    return (
        (pltpu.roll(plane, 1, 0) + pltpu.roll(plane, NY - 1, 0))
        + (pltpu.roll(plane, 1, 1) + pltpu.roll(plane, NZ - 1, 1))
    )


def kernel(
    n_domain, scale,
    x_hbm, v_hbm,
    y_ref, g_ref,
    xs, vs, ws, zst, hst, halo_out, halo_in, zall, lhs, gsum, rsb, zb, fin,
    lsem, xss, xrs, vss, vrs, hss, hrs, bss, brs, fss, frs, rss, rrs, zss, zrs, ass, ars, tokens,
):
    n_z = n_domain // GROUP
    d = lax.axis_index("domain")
    b = lax.axis_index("band")
    z, j = d // GROUP, d % GROUP
    x, h = b // 2, b % 2

    def at_d(step):
        return (lax.rem(d + step + n_domain, n_domain), b)

    def at_g(step):
        return (z * GROUP + lax.rem(j + step + GROUP, GROUP), b)

    def at_z(step):
        return (lax.rem(z + step + n_z, n_z) * GROUP + j, b)

    def at_b(dx, dh):
        return (d, lax.rem(x + dx + 4, 4) * 2 + lax.rem(h + dh, 2))

    def remote(src, dst, send, recv, to):
        return pltpu.make_async_remote_copy(
            src_ref=src, dst_ref=dst, send_sem=send, recv_sem=recv, device_id=to, device_id_type=MESH
        )

    own = pltpu.make_async_copy(x_hbm, xs.at[2], lsem.at[0])
    own_v = pltpu.make_async_copy(v_hbm, vs.at[2], lsem.at[1])
    own.start()
    own_v.start()
    barrier = pltpu.get_barrier_semaphore()
    partners = [at_d(s) for s in (-2, -1, 1, 2)] + [at_g(s) for s in range(1, GROUP)] + [at_z(-1), at_z(1)]
    partners += [at_b(0, 1), at_b(1, 0), at_b(-1, 0), at_b(2, 0)]
    for to in partners:
        pl.semaphore_signal(barrier, inc=1, device_id=to, device_id_type=MESH)
    own.wait()
    own_v.wait()
    pl.semaphore_wait(barrier, len(partners))

    def greet(n):
        for to in (at_z(-(1 << n)), at_z(1 << n)):
            pl.semaphore_signal(tokens.at[n], inc=1, device_id=to, device_id_type=MESH)

    def greeted(n):
        pl.semaphore_wait(tokens.at[n], 2)

    greet(0)

    pending = []
    shifts = (-1, 1, -2, 2)
    v_in = []
    for n, s in enumerate(shifts):
        cp = remote(vs.at[2], vs.at[2 - s], vss.at[n], vrs.at[n], at_d(s))
        cp.start()
        v_in.append(cp)
    pending += v_in
    size = NB // CHUNKS
    x_in = []
    for c in range(CHUNKS):
        part = pl.ds(c * size, size)
        x_in.append([])
        for n, s in enumerate(shifts):
            cp = remote(xs.at[2, part], xs.at[2 - s, part], xss.at[n, c], xrs.at[n, c], at_d(s))
            cp.start()
            x_in[c].append(cp)
        pending += x_in[c]

    center, terms = filter_terms()
    for cp in v_in:
        cp.wait_recv()
    for k, (alpha, _) in enumerate(terms):
        for p in range(k + 1, 9 - k):
            ws[k, p] = alpha * (vs[p // 2, (p % 2) * NY:(p % 2) * NY + NY, :] + (3.0 - center))

    def filter_some(i, _):
        orbitals = [i * BATCH + q for q in range(BATCH)]
        priors, currents = [], [None] * BATCH
        for o in orbitals:
            planes = {}
            for s in range(5):
                block = xs[s, o].astype(F32)
                planes[2 * s], planes[2 * s + 1] = block[:NY], block[NY:]
            priors.append(planes)
        for k, (alpha, beta) in enumerate(terms):
            for q in range(BATCH):
                base = currents[q] if k else priors[q]
                update = {}
                for p in range(k + 1, 9 - k):
                    near = side_sum(base[p]) + (base[p - 1] + base[p + 1])
                    value = ws[k, p] * base[p] - (0.5 * alpha) * near
                    if k:
                        value = value - beta * priors[q][p]
                    update[p] = value
                if k:
                    priors[q] = currents[q]
                currents[q] = update
        for q, o in enumerate(orbitals):
            low, high = currents[q][4], currents[q][5]
            zst[0, pl.ds(o, NY, stride=NB), :] = low
            zst[1, pl.ds(o, NY, stride=NB), :] = high
            y_ref[o] = jnp.concatenate([low, high], axis=0).astype(BF16)
        for q in range(0, BATCH, 2):
            for side in range(2):
                pair = [currents[q + r][4 + side] for r in range(2)]
                halo_out[side, i * (BATCH // 2) + q // 2] = jnp.concatenate(pair, axis=0).astype(BF16)
        return 0

    me = 32 * b
    mate = 32 * (x * 2 + (1 - h))
    x_steps = (1, -1, 2)
    half = NB // HALVES
    band_in, fwd_in, mate_in = [], [], []

    def band_piece(start, t, u):
        rows = pl.ds(pl.multiple_of(start + t * half, 16), half)
        return zall.at[u * (NY // SPLIT):(u + 1) * (NY // SPLIT), rows, :]

    for t in range(HALVES):
        for c in range(t * CHUNKS // HALVES, (t + 1) * CHUNKS // HALVES):
            for cp in x_in[c]:
                cp.wait_recv()
            lax.fori_loop(c * size // BATCH, (c + 1) * size // BATCH, filter_some, 0)
        rows = pl.ds(pl.multiple_of(me + t * half, 16), half)
        for y in range(NY):
            for p in range(2):
                piece = zst[p, y * NB + t * half:y * NB + (t + 1) * half, :].astype(BF16)
                zall[y, rows, p * NZ:(p + 1) * NZ] = piece
                lhs[y, t * half:(t + 1) * half, p * NZ:(p + 1) * NZ] = piece
        for u in range(SPLIT):
            piece = band_piece(me, t, u)
            cp = remote(piece, piece, bss.at[0, t, u], brs.at[0, t, u], at_b(0, 1))
            cp.start()
            mate_in.append(cp)
        if MATE_FIRST and t < HALVES - 1:
            continue
        for tt in range(HALVES) if MATE_FIRST else (t,):
            for u in range(SPLIT):
                piece = band_piece(me, tt, u)
                for n, s in enumerate(x_steps):
                    cp = remote(piece, piece, bss.at[n + 1, tt, u], brs.at[n + 1, tt, u], at_b(s, 0))
                    cp.start()
                    band_in.append(cp)
    pending += mate_in + band_in

    h_in = []
    for n, s in enumerate((-1, 1)):
        cp = remote(halo_out.at[n], halo_in.at[1 - n], hss.at[n], hrs.at[n], at_d(s))
        cp.start()
        h_in.append(cp)
    pending += h_in

    greeted(0)
    greet(1)
    for t in range(HALVES):
        for u in range(SPLIT):
            mate_in[t * SPLIT + u].wait_recv()
            piece = band_piece(mate, t, u)
            for n, s in enumerate(x_steps):
                cp = remote(piece, piece, fss.at[n, t, u], frs.at[n, t, u], at_b(s, 0))
                cp.start()
                fwd_in.append(cp)
    pending += fwd_in

    for cp in h_in:
        cp.wait_recv()

    def apply_pair(i, _):
        left, right = halo_in[0, i].astype(F32), halo_in[1, i].astype(F32)
        for q in range(2):
            o = 2 * i + q
            block = y_ref[o].astype(F32)
            planes = (left[q * NY:(q + 1) * NY], block[:NY], block[NY:], right[q * NY:(q + 1) * NY])
            for p in (1, 2):
                near = (planes[p - 1] + planes[p + 1]) + side_sum(planes[p])
                value = -0.5 * (near - 6.0 * planes[p]) + vs[2, (p - 1) * NY:p * NY, :] * planes[p]
                hst[p - 1, pl.ds(o, NY, stride=NB), :] = value
        return 0

    lax.fori_loop(0, NB // 2, apply_pair, 0)
    for y in range(NY):
        for p in range(2):
            lhs[y, NB:2 * NB, p * NZ:(p + 1) * NZ] = hst[p, y * NB:(y + 1) * NB, :].astype(BF16)

    greeted(1)
    greet(2)
    for cp in band_in + fwd_in:
        cp.wait_recv()
    total = None
    for y in range(NY):
        term = lax.dot_general(lhs[y], zall[y], (((1,), (1,)), ((), ())), preferred_element_type=F32)
        total = term if total is None else total + term
    gsum[...] = total

    r_in = []
    for s in range(1, GROUP):
        there = lax.rem(j + s, GROUP)
        cp = remote(gsum.at[pl.ds(pl.multiple_of(there * 8, 8), 8)], rsb.at[s], rss.at[s], rrs.at[s], at_g(s))
        cp.start()
        r_in.append(cp)
    pending += r_in
    mine = pl.ds(pl.multiple_of(j * 8, 8), 8)
    shard = gsum[mine, :]
    for s in range(1, GROUP):
        r_in[s - 1].wait_recv()
        shard = shard + rsb[s]
    zb[z] = jnp.concatenate([shard[:, :128], shard[:, 128:]], axis=0).astype(BF16)

    greeted(2)
    z_in = []
    for s in sorted(range(1, n_z), key=lambda s: -min(s, n_z - s)):
        cp = remote(zb.at[z], zb.at[z], zss.at[s], zrs.at[s], at_z(s))
        cp.start()
        z_in.append(cp)
    for cp in z_in:
        cp.wait_recv()
    pending += z_in
    values = [zb[k].astype(F32) for k in range(n_z)]
    while len(values) > 1:
        values = [values[k] + values[k + 1] for k in range(0, len(values), 2)]
    result = values[0] * scale
    fin[mine, :] = jnp.concatenate([result[:8], result[8:]], axis=1)

    a_in = []
    for s in range(1, GROUP):
        cp = remote(fin.at[mine], fin.at[mine], ass.at[s], ars.at[s], at_g(s))
        cp.start()
        a_in.append(cp)
    for cp in a_in:
        cp.wait_recv()
    pending += a_in
    g_ref[...] = fin[...]
    for cp in pending:
        cp.wait_send()


def shards(orbitals, potential, n_domain, n_band):
    n_z = n_domain // GROUP
    block = orbitals.reshape(NB, 2 * NY, NZ)
    scale = 1.0 / (n_domain * 2 * NY * NZ)
    dma = pltpu.SemaphoreType.DMA
    vmem = pl.BlockSpec(memory_space=pltpu.VMEM)
    filtered, rows = pl.pallas_call(
        functools.partial(kernel, n_domain, scale),
        out_shape=(
            jax.ShapeDtypeStruct((NB, 2 * NY, NZ), BF16),
            jax.ShapeDtypeStruct((2 * NB, n_band * NB), F32),
        ),
        in_specs=[pl.BlockSpec(memory_space=pltpu.HBM)] * 2,
        out_specs=(vmem, vmem),
        scratch_shapes=[
            pltpu.VMEM((5, NB, 2 * NY, NZ), BF16),
            pltpu.VMEM((5, 2 * NY, NZ), F32),
            pltpu.VMEM((4, 10, NY, NZ), F32),
            pltpu.VMEM((2, NY * NB, NZ), F32),
            pltpu.VMEM((2, NY * NB, NZ), F32),
            pltpu.VMEM((2, NB // 2, 2 * NY, NZ), BF16),
            pltpu.VMEM((2, NB // 2, 2 * NY, NZ), BF16),
            pltpu.VMEM((NY, n_band * NB, 2 * NZ), BF16),
            pltpu.VMEM((NY, 2 * NB, 2 * NZ), BF16),
            pltpu.VMEM((2 * NB, n_band * NB), F32),
            pltpu.VMEM((GROUP, 8, n_band * NB), F32),
            pltpu.VMEM((n_z, 16, n_band * NB // 2), BF16),
            pltpu.VMEM((2 * NB, n_band * NB), F32),
            dma((2,)),
            dma((4, CHUNKS)), dma((4, CHUNKS)),
            dma((4,)), dma((4,)),
            dma((2,)), dma((2,)),
            dma((4, HALVES, SPLIT)), dma((4, HALVES, SPLIT)),
            dma((3, HALVES, SPLIT)), dma((3, HALVES, SPLIT)),
            dma((GROUP,)), dma((GROUP,)),
            dma((n_z,)), dma((n_z,)),
            dma((GROUP,)), dma((GROUP,)),
            pltpu.SemaphoreType.REGULAR((3,)),
        ],
        compiler_params=pltpu.CompilerParams(
            collective_id=1, has_side_effects=True, vmem_limit_bytes=24 * 1024 * 1024
        ),
    )(*(pltpu.with_memory_space_constraint(a, pltpu.HBM) for a in (block, potential.reshape(2 * NY, NZ))))
    return filtered.reshape(orbitals.shape), rows[:NB], rows[NB:]


def solution(mesh):
    body = functools.partial(shards, n_domain=mesh.shape["domain"], n_band=mesh.shape["band"])
    in_specs = (P("band", "domain", None, None), P("domain", None, None))
    out_specs = (P("band", "domain", None, None), P("band", None), P("band", None))
    return jax.shard_map(body, mesh=mesh, in_specs=in_specs, out_specs=out_specs, check_vma=False)
```

```python
import functools

import jax
import jax.numpy as jnp
from jax import lax
from jax.experimental import pallas as pl
from jax.experimental.pallas import tpu as pltpu
from jax.sharding import PartitionSpec as P

MESH = pl.DeviceIdType.MESH
LOWER = -1.0
CUTOFF = 1.0
UPPER = 7.5
F32 = jnp.float32
BF16 = jnp.bfloat16
GROUP = 8
NB = 32
NY = 8
NZ = 128
CHUNKS = 4
HALVES = 2
SPLIT = 2
MATE_FIRST = False
BATCH = 4


def filter_terms():
    half_width = (UPPER - CUTOFF) / 2.0
    center = (UPPER + CUTOFF) / 2.0
    sigma = half_width / (LOWER - center)
    gamma = 2.0 / sigma
    terms = [(sigma / half_width, 0.0)]
    for step in range(3):
        sigma_next = 1.0 / (gamma - sigma)
        terms.append((2.0 * sigma_next / half_width, sigma * sigma_next))
        sigma = sigma_next
    return center, terms


def side_sum(plane):
    return (
        (pltpu.roll(plane, 1, 0) + pltpu.roll(plane, NY - 1, 0))
        + (pltpu.roll(plane, 1, 1) + pltpu.roll(plane, NZ - 1, 1))
    )


def kernel(
    n_domain, scale,
    x_hbm, v_hbm,
    y_ref, g_ref,
    xs, vs, ws, zst, hst, halo_out, halo_in, zall, lhs, gsum, gsend, rsb, zb, fin,
    lsem, xss, xrs, vss, vrs, hss, hrs, bss, brs, fss, frs, rss, rrs, zss, zrs, ass, ars, tokens,
):
    n_z = n_domain // GROUP
    d = lax.axis_index("domain")
    b = lax.axis_index("band")
    z, j = d // GROUP, d % GROUP
    x, h = b // 2, b % 2

    def at_d(step):
        return (lax.rem(d + step + n_domain, n_domain), b)

    def at_g(step):
        return (z * GROUP + lax.rem(j + step + GROUP, GROUP), b)

    def at_z(step):
        return (lax.rem(z + step + n_z, n_z) * GROUP + j, b)

    def at_b(dx, dh):
        return (d, lax.rem(x + dx + 4, 4) * 2 + lax.rem(h + dh, 2))

    def remote(src, dst, send, recv, to):
        return pltpu.make_async_remote_copy(
            src_ref=src, dst_ref=dst, send_sem=send, recv_sem=recv, device_id=to, device_id_type=MESH
        )

    own = pltpu.make_async_copy(x_hbm, xs.at[2], lsem.at[0])
    own_v = pltpu.make_async_copy(v_hbm, vs.at[2], lsem.at[1])
    own.start()
    own_v.start()
    barrier = pltpu.get_barrier_semaphore()
    partners = [at_d(s) for s in (-2, -1, 1, 2)] + [at_g(s) for s in range(1, GROUP)] + [at_z(-1), at_z(1)]
    partners += [at_b(0, 1), at_b(1, 0), at_b(-1, 0), at_b(2, 0)]
    for to in partners:
        pl.semaphore_signal(barrier, inc=1, device_id=to, device_id_type=MESH)
    own.wait()
    own_v.wait()
    pl.semaphore_wait(barrier, len(partners))

    def greet(n):
        for to in (at_z(-(1 << n)), at_z(1 << n)):
            pl.semaphore_signal(tokens.at[n], inc=1, device_id=to, device_id_type=MESH)

    def greeted(n):
        pl.semaphore_wait(tokens.at[n], 2)

    greet(0)

    pending = []
    shifts = (-1, 1, -2, 2)
    v_in = []
    for n, s in enumerate(shifts):
        cp = remote(vs.at[2], vs.at[2 - s], vss.at[n], vrs.at[n], at_d(s))
        cp.start()
        v_in.append(cp)
    pending += v_in
    size = NB // CHUNKS
    x_in = []
    for c in range(CHUNKS):
        part = pl.ds(c * size, size)
        x_in.append([])
        for n, s in enumerate(shifts):
            cp = remote(xs.at[2, part], xs.at[2 - s, part], xss.at[n, c], xrs.at[n, c], at_d(s))
            cp.start()
            x_in[c].append(cp)
        pending += x_in[c]

    center, terms = filter_terms()
    for cp in v_in:
        cp.wait_recv()
    for k, (alpha, _) in enumerate(terms):
        for p in range(k + 1, 9 - k):
            ws[k, p] = alpha * (vs[p // 2, (p % 2) * NY:(p % 2) * NY + NY, :] + (3.0 - center))

    def filter_some(i, _):
        orbitals = [i * BATCH + q for q in range(BATCH)]
        priors, currents = [], [None] * BATCH
        for o in orbitals:
            planes = {}
            for s in range(5):
                block = xs[s, o].astype(F32)
                planes[2 * s], planes[2 * s + 1] = block[:NY], block[NY:]
            priors.append(planes)
        for k, (alpha, beta) in enumerate(terms):
            for q in range(BATCH):
                base = currents[q] if k else priors[q]
                update = {}
                for p in range(k + 1, 9 - k):
                    near = side_sum(base[p]) + (base[p - 1] + base[p + 1])
                    value = ws[k, p] * base[p] - (0.5 * alpha) * near
                    if k:
                        value = value - beta * priors[q][p]
                    update[p] = value
                if k:
                    priors[q] = currents[q]
                currents[q] = update
        for q, o in enumerate(orbitals):
            low, high = currents[q][4], currents[q][5]
            zst[0, pl.ds(o, NY, stride=NB), :] = low
            zst[1, pl.ds(o, NY, stride=NB), :] = high
            y_ref[o] = jnp.concatenate([low, high], axis=0).astype(BF16)
        for q in range(0, BATCH, 2):
            for side in range(2):
                pair = [currents[q + r][4 + side] for r in range(2)]
                halo_out[side, i * (BATCH // 2) + q // 2] = jnp.concatenate(pair, axis=0).astype(BF16)
        return 0

    me = 32 * b
    mate = 32 * (x * 2 + (1 - h))
    x_steps = (1, -1, 2)
    half = NB // HALVES
    band_in, fwd_in, mate_in = [], [], []

    def band_piece(start, t, u):
        rows = pl.ds(pl.multiple_of(start + t * half, 16), half)
        return zall.at[u * (NY // SPLIT):(u + 1) * (NY // SPLIT), rows, :]

    for t in range(HALVES):
        for c in range(t * CHUNKS // HALVES, (t + 1) * CHUNKS // HALVES):
            for cp in x_in[c]:
                cp.wait_recv()
            lax.fori_loop(c * size // BATCH, (c + 1) * size // BATCH, filter_some, 0)
        rows = pl.ds(pl.multiple_of(me + t * half, 16), half)
        for y in range(NY):
            for p in range(2):
                piece = zst[p, y * NB + t * half:y * NB + (t + 1) * half, :].astype(BF16)
                zall[y, rows, p * NZ:(p + 1) * NZ] = piece
                lhs[y, t * half:(t + 1) * half, p * NZ:(p + 1) * NZ] = piece
        for u in range(SPLIT):
            piece = band_piece(me, t, u)
            cp = remote(piece, piece, bss.at[0, t, u], brs.at[0, t, u], at_b(0, 1))
            cp.start()
            mate_in.append(cp)
        if MATE_FIRST and t < HALVES - 1:
            continue
        for tt in range(HALVES) if MATE_FIRST else (t,):
            for u in range(SPLIT):
                piece = band_piece(me, tt, u)
                for n, s in enumerate(x_steps):
                    cp = remote(piece, piece, bss.at[n + 1, tt, u], brs.at[n + 1, tt, u], at_b(s, 0))
                    cp.start()
                    band_in.append(cp)
    pending += mate_in + band_in

    h_in = []
    for n, s in enumerate((-1, 1)):
        cp = remote(halo_out.at[n], halo_in.at[1 - n], hss.at[n], hrs.at[n], at_d(s))
        cp.start()
        h_in.append(cp)
    pending += h_in

    greeted(0)
    greet(1)
    for t in range(HALVES):
        for u in range(SPLIT):
            mate_in[t * SPLIT + u].wait_recv()
            piece = band_piece(mate, t, u)
            for n, s in enumerate(x_steps):
                cp = remote(piece, piece, fss.at[n, t, u], frs.at[n, t, u], at_b(s, 0))
                cp.start()
                fwd_in.append(cp)
    pending += fwd_in

    for cp in h_in:
        cp.wait_recv()

    def apply_pair(i, _):
        left, right = halo_in[0, i].astype(F32), halo_in[1, i].astype(F32)
        for q in range(2):
            o = 2 * i + q
            block = y_ref[o].astype(F32)
            planes = (left[q * NY:(q + 1) * NY], block[:NY], block[NY:], right[q * NY:(q + 1) * NY])
            for p in (1, 2):
                near = (planes[p - 1] + planes[p + 1]) + side_sum(planes[p])
                value = -0.5 * (near - 6.0 * planes[p]) + vs[2, (p - 1) * NY:p * NY, :] * planes[p]
                hst[p - 1, pl.ds(o, NY, stride=NB), :] = value
        return 0

    lax.fori_loop(0, NB // 2, apply_pair, 0)
    for y in range(NY):
        for p in range(2):
            lhs[y, NB:2 * NB, p * NZ:(p + 1) * NZ] = hst[p, y * NB:(y + 1) * NB, :].astype(BF16)

    greeted(1)
    greet(2)
    for cp in band_in + fwd_in:
        cp.wait_recv()
    total = None
    for y in range(NY):
        term = lax.dot_general(lhs[y], zall[y], (((1,), (1,)), ((), ())), preferred_element_type=F32)
        total = term if total is None else total + term
    for k in range(GROUP):
        rows = total[8 * k:8 * k + 8]
        packed = jnp.concatenate([rows[:, :128], rows[:, 128:]], axis=0)
        gsum[k] = packed
        gsend[k] = packed.astype(BF16)

    r_in = []
    for s in range(1, GROUP):
        there = lax.rem(j + s, GROUP)
        cp = remote(gsend.at[there], rsb.at[s], rss.at[s], rrs.at[s], at_g(s))
        cp.start()
        r_in.append(cp)
    pending += r_in
    mine = pl.ds(pl.multiple_of(j * 8, 8), 8)
    shard = gsum[j]
    for s in range(1, GROUP):
        r_in[s - 1].wait_recv()
        shard = shard + rsb[s].astype(F32)
    zb[z] = shard.astype(BF16)

    greeted(2)
    z_in = []
    for s in sorted(range(1, n_z), key=lambda s: -min(s, n_z - s)):
        cp = remote(zb.at[z], zb.at[z], zss.at[s], zrs.at[s], at_z(s))
        cp.start()
        z_in.append(cp)
    for cp in z_in:
        cp.wait_recv()
    pending += z_in
    values = [zb[k].astype(F32) for k in range(n_z)]
    while len(values) > 1:
        values = [values[k] + values[k + 1] for k in range(0, len(values), 2)]
    result = values[0] * scale
    fin[mine, :] = jnp.concatenate([result[:8], result[8:]], axis=1)

    a_in = []
    for s in range(1, GROUP):
        cp = remote(fin.at[mine], fin.at[mine], ass.at[s], ars.at[s], at_g(s))
        cp.start()
        a_in.append(cp)
    for cp in a_in:
        cp.wait_recv()
    pending += a_in
    g_ref[...] = fin[...]
    for cp in pending:
        cp.wait_send()


def shards(orbitals, potential, n_domain, n_band):
    n_z = n_domain // GROUP
    block = orbitals.reshape(NB, 2 * NY, NZ)
    scale = 1.0 / (n_domain * 2 * NY * NZ)
    dma = pltpu.SemaphoreType.DMA
    vmem = pl.BlockSpec(memory_space=pltpu.VMEM)
    filtered, rows = pl.pallas_call(
        functools.partial(kernel, n_domain, scale),
        out_shape=(
            jax.ShapeDtypeStruct((NB, 2 * NY, NZ), BF16),
            jax.ShapeDtypeStruct((2 * NB, n_band * NB), F32),
        ),
        in_specs=[pl.BlockSpec(memory_space=pltpu.HBM)] * 2,
        out_specs=(vmem, vmem),
        scratch_shapes=[
            pltpu.VMEM((5, NB, 2 * NY, NZ), BF16),
            pltpu.VMEM((5, 2 * NY, NZ), F32),
            pltpu.VMEM((4, 10, NY, NZ), F32),
            pltpu.VMEM((2, NY * NB, NZ), F32),
            pltpu.VMEM((2, NY * NB, NZ), F32),
            pltpu.VMEM((2, NB // 2, 2 * NY, NZ), BF16),
            pltpu.VMEM((2, NB // 2, 2 * NY, NZ), BF16),
            pltpu.VMEM((NY, n_band * NB, 2 * NZ), BF16),
            pltpu.VMEM((NY, 2 * NB, 2 * NZ), BF16),
            pltpu.VMEM((GROUP, 16, n_band * NB // 2), F32),
            pltpu.VMEM((GROUP, 16, n_band * NB // 2), BF16),
            pltpu.VMEM((GROUP, 16, n_band * NB // 2), BF16),
            pltpu.VMEM((n_z, 16, n_band * NB // 2), BF16),
            pltpu.VMEM((2 * NB, n_band * NB), F32),
            dma((2,)),
            dma((4, CHUNKS)), dma((4, CHUNKS)),
            dma((4,)), dma((4,)),
            dma((2,)), dma((2,)),
            dma((4, HALVES, SPLIT)), dma((4, HALVES, SPLIT)),
            dma((3, HALVES, SPLIT)), dma((3, HALVES, SPLIT)),
            dma((GROUP,)), dma((GROUP,)),
            dma((n_z,)), dma((n_z,)),
            dma((GROUP,)), dma((GROUP,)),
            pltpu.SemaphoreType.REGULAR((3,)),
        ],
        compiler_params=pltpu.CompilerParams(
            collective_id=1, has_side_effects=True, vmem_limit_bytes=24 * 1024 * 1024
        ),
    )(*(pltpu.with_memory_space_constraint(a, pltpu.HBM) for a in (block, potential.reshape(2 * NY, NZ))))
    return filtered.reshape(orbitals.shape), rows[:NB], rows[NB:]


def solution(mesh):
    body = functools.partial(shards, n_domain=mesh.shape["domain"], n_band=mesh.shape["band"])
    in_specs = (P("band", "domain", None, None), P("domain", None, None))
    out_specs = (P("band", "domain", None, None), P("band", None), P("band", None))
    return jax.shard_map(body, mesh=mesh, in_specs=in_specs, out_specs=out_specs, check_vma=False)
```
